32 devices in a mesh: stream: 4 (over y, x), span: 8 (over z, core).
Axes of the slice: x: 2, y: 2, z: 4, core: 2. Of those that a mesh axis runs over, the one named last changes fastest.
Arguments:
- perturbation: float32 [5, 128, 512, 128], P(None, 'stream', 'span'), may hold values from -6 to 6
- base_flow: float32 [4, 128, 512, 128], P(None, 'stream', 'span'), may hold values from -1 to 1.2, as said below
- donor_stream: int32 [4, 2048], P('stream', 'span'), may hold values from 0 to 30
- donor_span: int32 [4, 2048], P('stream', 'span'), may hold values from 0 to 62
- donor_weights: float32 [3, 4, 2048], P(None, 'stream', 'span'), may hold values from 0 to 1
- donor_receiver: int32 [4, 2048], P('stream', 'span'), may hold values from 0 to 7, as said below
- target_stream: int32 [4, 2048], P('stream', 'span'), may hold values from 4 to 27
- target_span: int32 [4, 2048], P('stream', 'span'), may hold values from 4 to 59
Outputs:
- advanced: float32 [5, 128, 512, 128], P(None, 'stream', 'span')
The draws below stay inside these ranges and needn't reach their ends.
Inputs may be any that keep to these rules, and one draw needn't show every extreme that they name: `donor_receiver`: in every streamwise row one spanwise block receives exactly 64 tiles from every block of the row, and no block sends more than 64 tiles to one receiving block. `base_flow`: component 0 lies in 0.4 to 1.2, component 1 in -0.4 to 0.4, component 2 in 0.5 to 1.0, component 3 in -1 to 1.
All inputs are finite; a program needn't handle non-finite values.
Results may differ from the reference program's by a relative error of at most 0.000073.
Values sent between devices are 32-bit elements; how exact they have to be, the bound alone decides.
A program may use at most 256 MiB of HBM per device.

```python
import jax
import jax.numpy as jnp
from jax import lax

CX = 32
CZ = 64
CY = 128
DONORS = 256
CAP = 64
SX = 4
SPANS = 8
NX = 128
NZ = 512
ENTRIES = 2048


def draw_base_flow(key, part):
    keys = jax.random.split(key, 4)
    lowest = (0.4, -0.4, 0.5, -1.0)
    highest = (1.2, 0.4, 1.0, 1.0)
    fields = []
    for index in range(4):
        fraction = jax.random.uniform(keys[index], (NX, NZ, CY), jnp.float32)
        fields.append(lowest[index] + (highest[index] - lowest[index]) * fraction)
    return jnp.stack(fields).astype(jnp.float32)


def draw_donor_receiver(key, part):
    hot_rows = jax.random.randint(jax.random.fold_in(key, 11), (SX,), 0, SPANS)
    device_keys = jax.random.split(jax.random.fold_in(key, 12), SX * SPANS)
    hot_each = jnp.repeat(hot_rows, SPANS)

    def one_device(device_key, hottest):
        order_key, offset_key = jax.random.split(device_key)
        offset = jax.random.randint(offset_key, (), 0, SPANS - 1)
        entry = jnp.arange(DONORS, dtype=jnp.int32)
        others = (hottest + 1 + (offset + entry) % (SPANS - 1)) % SPANS
        chosen = jnp.where(entry < CAP, hottest, others)
        return jax.random.permutation(order_key, chosen)
    return jax.vmap(one_device)(device_keys, hot_each).reshape(SX, ENTRIES).astype(jnp.int32)


def with_ends(drawn, key, low, high):
    longest = drawn.shape.index(max(drawn.shape))
    spots = []
    for shift in (0, 1):
        where = [jax.random.randint(jax.random.fold_in(key, axis), (), 0, length) for axis, length in enumerate(drawn.shape)]
        where[longest] = (where[longest] + shift) % drawn.shape[longest]
        spots.append(tuple(where))
    return drawn.at[spots[0]].set(low).at[spots[1]].set(high)


def level_of(own_key, shape, shards, least, high):
    def one(dim, shards_of):
        heights = jax.random.uniform(jax.random.fold_in(jax.random.fold_in(own_key, 6), dim), (shards_of,), jnp.float32, least / len(shards), high / len(shards))
        return jnp.repeat(jnp.exp(heights), shape[dim] // shards_of).reshape((-1,) + (1,) * (len(shape) - dim - 1))

    level = one(*shards[0])
    for cut in shards[1:]:
        level = level * one(*cut)
    return level


def scatter_about(own_key, shape, width, limit, cuts=(), kind=jnp.bfloat16):
    array = jax.random.normal(own_key, shape, jnp.float32) * width
    if len(cuts) > 0:
        array = level_of(own_key, shape, cuts, -0.22, 0.18) * array
    return jnp.clip(array, min=-limit, max=limit).astype(kind)


def setup_inputs(seed: int = 0) -> dict:
    streams_of = jax.random.split(jax.random.key(seed), 9)
    return {
        "perturbation": scatter_about(streams_of[0], (5, NX, NZ, CY), 1.0, 6.0, ((1, 4), (2, 8)), jnp.float32),
        "base_flow": draw_base_flow(jax.random.fold_in(streams_of[8], 71), 0),
        "donor_stream": with_ends(jax.random.randint(streams_of[2], (SX, ENTRIES), 0, CX - 1), jax.random.fold_in(streams_of[2], 1), 0, (CX - 1) - 1).astype(jnp.int32),
        "donor_span": with_ends(jax.random.randint(streams_of[3], (SX, ENTRIES), 0, CZ - 1), jax.random.fold_in(streams_of[3], 1), 0, (CZ - 1) - 1).astype(jnp.int32),
        "donor_weights": jnp.clip(1.0 * jax.random.uniform(streams_of[4], (3, SX, ENTRIES), jnp.float32) ** level_of(streams_of[4], (3, SX, ENTRIES), ((1, 4), (2, 8)), -0.2, 0.2), 0.0, 1.0),
        "donor_receiver": draw_donor_receiver(jax.random.fold_in(streams_of[8], 71), 0),
        "target_stream": with_ends(jax.random.randint(streams_of[6], (SX, ENTRIES), 4, CX - 4), jax.random.fold_in(streams_of[6], 1), 4, (CX - 4) - 1).astype(jnp.int32),
        "target_span": with_ends(jax.random.randint(streams_of[7], (SX, ENTRIES), 4, CZ - 4), jax.random.fold_in(streams_of[7], 1), 4, (CZ - 4) - 1).astype(jnp.int32),
    }


viscosity = 0.02
penalty_rate = 1.5
time_step = 0.25


def first_diff(padded, dimension, extent):
    lower_two = lax.slice_in_dim(padded, 0, extent, axis=dimension)
    lower_one = lax.slice_in_dim(padded, 1, extent + 1, axis=dimension)
    upper_one = lax.slice_in_dim(padded, 3, extent + 3, axis=dimension)
    upper_two = lax.slice_in_dim(padded, 4, extent + 4, axis=dimension)
    return (lower_two - 8.0 * lower_one + 8.0 * upper_one - upper_two) / 12.0


def second_diff(padded, dimension, extent):
    lower_two = lax.slice_in_dim(padded, 0, extent, axis=dimension)
    lower_one = lax.slice_in_dim(padded, 1, extent + 1, axis=dimension)
    middle = lax.slice_in_dim(padded, 2, extent + 2, axis=dimension)
    upper_one = lax.slice_in_dim(padded, 3, extent + 3, axis=dimension)
    upper_two = lax.slice_in_dim(padded, 4, extent + 4, axis=dimension)
    return (-lower_two + 16.0 * lower_one - 30.0 * middle + 16.0 * upper_one - upper_two) / 12.0


def operator_part(center, stream_wide, span_wide, flow_block):
    stream_cells = center.shape[1]
    span_cells = center.shape[2]
    normal_cells = center.shape[3]
    normal_wide = jnp.pad(center, ((0, 0), (0, 0), (0, 0), (2, 2)))
    stream_grad = first_diff(stream_wide, 1, stream_cells)
    span_grad = first_diff(span_wide, 2, span_cells)
    wall_grad_velocity = first_diff(normal_wide[2], 2, normal_cells)
    wall_grad_pressure = first_diff(normal_wide[4], 2, normal_cells)
    laplace = second_diff(stream_wide, 1, stream_cells) + second_diff(span_wide, 2, span_cells) + second_diff(normal_wide, 3, normal_cells)
    tendency = viscosity * laplace - (flow_block[0] * stream_grad + flow_block[1] * span_grad)
    acoustic = flow_block[2]
    components = [
        tendency[0],
        tendency[1] - acoustic * stream_grad[4] - flow_block[3] * center[2],
        tendency[2] - acoustic * wall_grad_pressure,
        tendency[3] - acoustic * span_grad[4],
        tendency[4] - acoustic * (stream_grad[1] + wall_grad_velocity + span_grad[3]),
    ]
    return jnp.stack(components)


def blend(corner00, corner10, corner01, corner11, stream_weight, span_weight, normal_weight):
    bilinear = ((1.0 - stream_weight) * (1.0 - span_weight) * corner00
                + stream_weight * (1.0 - span_weight) * corner10
                + (1.0 - stream_weight) * span_weight * corner01
                + stream_weight * span_weight * corner11)
    shifted = jnp.concatenate([bilinear[..., 1:], jnp.zeros_like(bilinear[..., :1])], axis=-1)
    return (1.0 - normal_weight) * bilinear + normal_weight * shifted


def widen(values, dimension, periodic):
    widths = [(0, 0)] * values.ndim
    widths[dimension] = (2, 2)
    if periodic:
        return jnp.pad(values, widths, mode="wrap")
    return jnp.pad(values, widths)


def reference(perturbation, base_flow, donor_stream, donor_span, donor_weights, donor_receiver, target_stream, target_span):
    row_block = jnp.arange(SX, dtype=jnp.int32)[:, None]
    span_block = (jnp.arange(ENTRIES, dtype=jnp.int32) // DONORS)[None, :]
    source_x = row_block * CX + donor_stream
    source_z = span_block * CZ + donor_span
    target_x = row_block * CX + target_stream
    target_z = donor_receiver * CZ + target_span
    stream_weight = donor_weights[0][None, :, :, None]
    span_weight = donor_weights[1][None, :, :, None]
    normal_weight = donor_weights[2][None, :, :, None]
    counted = jnp.zeros((NX, NZ), jnp.float32).at[target_x, target_z].add(1.0)[:, :, None]

    def donor_term(current):
        values = blend(current[:, source_x, source_z, :], current[:, source_x + 1, source_z, :],
                       current[:, source_x, source_z + 1, :], current[:, source_x + 1, source_z + 1, :],
                       stream_weight, span_weight, normal_weight)
        return jnp.zeros_like(current).at[:, target_x, target_z, :].add(values)

    def tendency(current):
        streamwise = widen(current, 1, False)

        def block_rows(block_index):
            row_start = block_index * CX
            stream_wide = lax.dynamic_slice_in_dim(streamwise, row_start, CX + 4, 1)
            middle = stream_wide[:, 2:CX + 2]
            span_wide = widen(middle, 2, True)
            flow_block = lax.dynamic_slice_in_dim(base_flow, row_start, CX, 1)
            return operator_part(middle, stream_wide, span_wide, flow_block)

        blocks = lax.map(block_rows, jnp.arange(SX, dtype=jnp.int32))
        joined = jnp.transpose(blocks, (1, 0, 2, 3, 4)).reshape(5, NX, NZ, CY)
        return joined + penalty_rate * (donor_term(current) - counted * current)

    section_one = perturbation + time_step * tendency(perturbation)
    section_two = 0.75 * perturbation + 0.25 * (section_one + time_step * tendency(section_one))
    return perturbation / 3.0 + 2.0 / 3.0 * (section_two + time_step * tendency(section_two))
```

```python
import functools

import jax
import jax.numpy as jnp
from jax import lax
from jax.experimental import pallas as pl
from jax.experimental.pallas import tpu as pltpu
from jax.sharding import PartitionSpec as P

viscosity = 0.02
penalty_rate = 1.5
time_step = 0.25
MESH = pl.DeviceIdType.MESH
F32 = jnp.float32
BF16 = jnp.bfloat16


def split(values):
    high = values.astype(BF16)
    low = (values - high.astype(F32)).astype(BF16)
    return high, low


def kernel(
    rows, spans, X, Z, donors, cap,
    pert, flow_in, meta, out,
    q, flow, send, recv, zsend, zrecv, tsend, trecv,
    a_high, a_low, wy, landing, counted, trow, qcat, band, ybuf,
    load_sem, out_sem, send_sem, recv_sem, xs_sem, xr_sem, zs_sem, zr_sem, ts_sem, tr_sem,
):
    sx = lax.axis_index("stream")
    me = lax.axis_index("span")
    Y = 128
    slots = spans * cap

    def load(f):
        return pltpu.make_async_copy(
            pert.at[f], q.at[0, f, pl.ds(2, X), pl.ds(8, Z), :], load_sem.at[f])

    flow_load = pltpu.make_async_copy(flow_in, flow, load_sem.at[5])
    for f in range(5):
        load(f).start()
    flow_load.start()

    barrier = pltpu.get_barrier_semaphore()
    for k in range(1, spans):
        pl.semaphore_signal(barrier, inc=1, device_id=(sx, lax.rem(me + k, spans)), device_id_type=MESH)

    for k in (1, rows - 1):
        pl.semaphore_signal(barrier, inc=1, device_id=(lax.rem(sx + k, rows), me), device_id_type=MESH)
    pl.semaphore_wait(barrier, spans + 1)

    @pl.when(sx == 0)
    def _():
        for s in range(3):
            for f in range(5):
                q[s, f, 0:2, 8:8 + Z, :] = jnp.zeros((2, Z, Y), F32)

    @pl.when(sx == rows - 1)
    def _():
        for s in range(3):
            for f in range(5):
                q[s, f, X + 2:X + 4, 8:8 + Z, :] = jnp.zeros((2, Z, Y), F32)

    r = lax.broadcasted_iota(jnp.int32, (2 * Y, Y), 0) % Y
    c = lax.broadcasted_iota(jnp.int32, (2 * Y, Y), 1)
    gap = r - c
    near = jnp.abs(gap) == 1
    far = jnp.abs(gap) == 2
    band[:, 0:Y] = jnp.where(gap == 0, -30.0, jnp.where(near, 16.0, jnp.where(far, -1.0, 0.0))).astype(BF16)
    sign = jnp.where(gap > 0, 1.0, -1.0)
    band[:, Y:2 * Y] = (jnp.where(near, 8.0, jnp.where(far, -1.0, 0.0)) * sign).astype(BF16)

    dest_row = meta[0:1, :]
    source_row = meta[1:2, :]
    fx_row = meta[2:3, :]
    fz_row = meta[3:4, :]
    fy_row = meta[4:5, :]
    target_row = meta[5:6, :]
    e_col = lax.broadcasted_iota(jnp.int32, (donors, donors), 0)
    e_row = lax.broadcasted_iota(jnp.int32, (donors, donors), 1)

    def to_col(row):
        return jnp.sum(jnp.where(e_col == e_row, row, 0.0), axis=1, keepdims=True)

    dest_col = to_col(dest_row)
    target_col = to_col(target_row)
    same = dest_col == dest_row
    rank_row = jnp.sum(jnp.where(same & (e_col < e_row), 1.0, 0.0), axis=0, keepdims=True)
    rank_col = jnp.sum(jnp.where(same & (e_row < e_col), 1.0, 0.0), axis=1, keepdims=True)
    position_row = dest_row * cap + rank_row
    lane = (lax.broadcasted_iota(jnp.int32, (donors, 128), 1) % cap).astype(F32)
    here = rank_col == lane
    for d in range(spans):
        picked = here & (dest_col == float(d))
        row = jnp.sum(jnp.where(picked, target_col + 1.0, 0.0), axis=0, keepdims=True) - 1.0
        tsend[d] = jnp.broadcast_to(row, (8, 128))

    def target_copy(peer, slot):
        return pltpu.make_async_remote_copy(
            src_ref=tsend.at[peer], dst_ref=trecv.at[slot], send_sem=ts_sem.at[peer],
            recv_sem=tr_sem.at[slot], device_id=(sx, peer), device_id_type=MESH)

    for k in range(1, spans):
        target_copy(lax.rem(me + k, spans), me).start()
    trecv[me] = tsend[me]

    @pl.loop(0, spans)
    def _(d):
        slot = (lax.broadcasted_iota(jnp.int32, (cap, donors), 0) + d * cap).astype(F32)
        mask = slot == position_row

        def pick(row):
            return jnp.sum(jnp.where(mask, row, 0.0), axis=1, keepdims=True)

        valid = pick(jnp.ones((1, donors), F32))
        source = pick(source_row).astype(jnp.int32)
        fx = pick(fx_row)
        fz = pick(fz_row)
        fy = pick(fy_row)
        wy[pl.ds(pl.multiple_of(d * cap, cap), cap), :] = jnp.broadcast_to(fy, (cap, Y))
        w00 = valid * (1.0 - fx) * (1.0 - fz)
        w10 = valid * fx * (1.0 - fz)
        w01 = valid * (1.0 - fx) * fz
        w11 = valid * fx * fz
        for j in range(X * Z // 256):
            col = lax.broadcasted_iota(jnp.int32, (cap, 256), 1) + j * 256 - source
            w = jnp.where(col == 0, w00, jnp.where(col == 1, w01, jnp.where(
                col == Z, w10, jnp.where(col == Z + 1, w11, 0.0))))
            high, low = split(w)
            a_high[pl.ds(pl.multiple_of(d * cap, cap), cap), j * 256:(j + 1) * 256] = high
            a_low[pl.ds(pl.multiple_of(d * cap, cap), cap), j * 256:(j + 1) * 256] = low

    for f in range(5):
        load(f).wait()

    def xcopy(s, side):
        first = 2 if side == 0 else X
        landed = X + 2 if side == 0 else 0
        peer = jnp.maximum(sx - 1, 0) if side == 0 else jnp.minimum(sx + 1, rows - 1)
        return pltpu.make_async_remote_copy(
            src_ref=q.at[s, :, pl.ds(first, 2), pl.ds(8, Z), :],
            dst_ref=q.at[s, :, pl.ds(landed, 2), pl.ds(8, Z), :],
            send_sem=xs_sem.at[side], recv_sem=xr_sem.at[s, side],
            device_id=(peer, me), device_id_type=MESH)

    def zcopy(s, side):
        peer = lax.rem(me + spans - 1, spans) if side == 0 else lax.rem(me + 1, spans)
        return pltpu.make_async_remote_copy(
            src_ref=zsend.at[side], dst_ref=zrecv.at[s, side],
            send_sem=zs_sem.at[side], recv_sem=zr_sem.at[s, side],
            device_id=(sx, peer), device_id_type=MESH)

    def tile_copy(s, f, peer, slot):
        return pltpu.make_async_remote_copy(
            src_ref=send.at[f, peer], dst_ref=recv.at[s, f, slot],
            send_sem=send_sem.at[f, peer], recv_sem=recv_sem.at[s, f, slot],
            device_id=(sx, peer), device_id_type=MESH)

    def land(s, f, target):
        @pl.loop(1, spans)
        def _(k):
            tile_copy(s, f, lax.rem(me + k, spans), lax.rem(me + k, spans)).wait_recv()
        scale = penalty_rate * time_step * jnp.where(s == 0, 1.0, jnp.where(s == 1, 0.25, 2.0 / 3.0))
        high, low = split(recv[s, f].reshape(slots, Y))
        rhs = jnp.concatenate([high, low], axis=1)
        group = 8 if (X - 8) % 8 == 0 else 4

        @pl.loop(0, (X - 8) // group)
        def _(g):
            part = landing[pl.ds(pl.multiple_of(g * group * Z, group * Z), group * Z), :]
            both = jnp.dot(part, rhs, preferred_element_type=F32)
            total = (both[:, 0:Y] + both[:, Y:2 * Y]) * scale
            for i in range(group):
                x = 6 + g * group + i
                q[target, f, x, 8:8 + Z, :] = q[target, f, x, 8:8 + Z, :] + total[i * Z:(i + 1) * Z]

    def interpolate(s, f):
        @pl.loop(0, X)
        def _(x):
            high, low = split(q[s, f, 2 + x, 8:8 + Z, :])
            at = pl.ds(pl.multiple_of(x * Z, Z), Z)
            qcat[at, 0:Y] = high
            qcat[at, Y:2 * Y] = low

        @pl.when(s > 0)
        def _():
            @pl.loop(1, spans)
            def _(k):
                tile_copy(s, f, lax.rem(me + k, spans), me).wait_send()

        block = 256

        @pl.loop(0, slots // block)
        def _(g):
            at = pl.ds(pl.multiple_of(g * block, block), block)
            both = jnp.dot(a_high[at, :], qcat[...], preferred_element_type=F32)
            rest = jnp.dot(a_low[at, :], qcat[:, 0:Y], preferred_element_type=F32)
            value = both[:, 0:Y] + both[:, Y:2 * Y] + rest
            lane = lax.broadcasted_iota(jnp.int32, (block, Y), 1)
            shifted = jnp.where(lane == Y - 1, 0.0, pltpu.roll(value, Y - 1, 1))
            value = value + wy[at, :] * (shifted - value)
            for i in range(block // cap):
                send[f, g * (block // cap) + i] = value[i * cap:(i + 1) * cap]

        @pl.loop(1, spans)
        def _(k):
            tile_copy(s, f, lax.rem(me + k, spans), me).start()
        recv[s, f, me] = send[f, me]

    def build_landing():
        for k in range(1, spans):
            peer = lax.rem(me + k, spans)
            target_copy(peer, peer).wait_recv()
        lane = lax.broadcasted_iota(jnp.int32, (8, 128), 1)
        for p in range(spans // 2):
            trow[:, p * 128:(p + 1) * 128] = jnp.where(lane < cap, trecv[2 * p], trecv[2 * p + 1])

        @pl.loop(0, X)
        def _(x):
            counted[x] = jnp.zeros((Z, Y), F32)

        @pl.loop(4, X - 4)
        def _(x):
            col = (lax.broadcasted_iota(jnp.int32, (Z, slots), 0) + x * Z).astype(F32)
            hit = jnp.where(col == trow[0:1, :], 1.0, 0.0)
            landing[pl.ds(pl.multiple_of((x - 4) * Z, Z), Z), :] = hit.astype(BF16)
            counted[x] = jnp.broadcast_to(jnp.sum(hit, axis=1, keepdims=True), (Z, Y))

    def stencil(s, target):
        ours = jnp.where(s == 0, 0.0, jnp.where(s == 1, 0.75, 1.0 / 3.0))
        kept = jnp.where(s == 0, 1.0, jnp.where(s == 1, 0.25, 2.0 / 3.0))
        rate = kept * time_step
        twelfth = rate * (1.0 / 12.0)
        nu = viscosity * twelfth
        tall = 16

        @pl.loop(0, X)
        def _(x):
            for f in range(5):
                high, low = split(q[s, f, 2 + x, 8:8 + Z, :])
                both = jnp.concatenate([high, low], axis=1)
                if f in (2, 4):
                    ybuf[f] = jnp.dot(both, band[...], preferred_element_type=F32)
                else:
                    ybuf[f, :, 0:Y] = jnp.dot(both, band[:, 0:Y], preferred_element_type=F32)

            @pl.loop(0, Z // tall)
            def _(t):
                z = t * tall
                zat = pl.ds(pl.multiple_of(z, tall), tall)
                stream_speed = flow[0, x, zat, :] * twelfth
                span_speed = flow[1, x, zat, :] * twelfth
                acoustic = flow[2, x, zat, :] * twelfth
                shear = flow[3, x, zat, :] * rate
                held = kept - (penalty_rate * rate) * counted[x, zat, :]
                result, dx, dz, mid = [], [], [], []
                for f in range(5):
                    def at(i, j):
                        return q[s, f, x + 2 + i, pl.ds(z + 8 + j, tall), :]
                    m = q[s, f, x + 2, pl.ds(pl.multiple_of(z + 8, 8), tall), :]
                    x0, x1, x3, x4 = at(-2, 0), at(-1, 0), at(1, 0), at(2, 0)
                    z0, z1, z3, z4 = at(0, -2), at(0, -1), at(0, 1), at(0, 2)
                    gx = 8.0 * (x3 - x1) - (x4 - x0)
                    gz = 8.0 * (z3 - z1) - (z4 - z0)
                    lap = 16.0 * ((x1 + x3) + (z1 + z3)) - ((x0 + x4) + (z0 + z4)) - 60.0 * m
                    lap = lap + ybuf[f, zat, 0:Y]
                    old = q[0, f, x + 2, pl.ds(pl.multiple_of(z + 8, 8), tall), :]
                    result.append(ours * old + held * m + nu * lap - stream_speed * gx - span_speed * gz)
                    dx.append(gx)
                    dz.append(gz)
                    mid.append(m)
                result[1] = result[1] - acoustic * dx[4] - shear * mid[2]
                result[2] = result[2] - acoustic * ybuf[4, zat, Y:2 * Y]
                result[3] = result[3] - acoustic * dz[4]
                result[4] = result[4] - acoustic * (dx[1] + ybuf[2, zat, Y:2 * Y] + dz[3])
                for f in range(5):
                    q[target, f, x + 2, pl.ds(pl.multiple_of(z + 8, 8), tall), :] = result[f]

    @pl.loop(0, 3)
    def _(s):
        @pl.when(sx > 0)
        def _():
            xcopy(s, 0).start()

        @pl.when(sx < rows - 1)
        def _():
            xcopy(s, 1).start()

        for f in range(5):
            @pl.loop(0, X)
            def _(x):
                at = pl.ds((f * X + x) * 2, 2)
                zsend[0, at, :] = q[s, f, x + 2, 8:10, :]
                zsend[1, at, :] = q[s, f, x + 2, Z + 6:Z + 8, :]
        zcopy(s, 0).start()
        zcopy(s, 1).start()

        @pl.loop(0, 5)
        def _(f):
            @pl.when(s > 0)
            def _():
                land(s - 1, f, s)
            interpolate(s, f)

        @pl.when(s == 0)
        def _():
            build_landing()
            flow_load.wait()

        zcopy(s, 0).wait()
        zcopy(s, 1).wait()
        for f in range(5):
            @pl.loop(0, X)
            def _(x):
                at = pl.ds((f * X + x) * 2, 2)
                q[s, f, x + 2, Z + 8:Z + 10, :] = zrecv[s, 0, at, :]
                q[s, f, x + 2, 6:8, :] = zrecv[s, 1, at, :]

        @pl.when(sx > 0)
        def _():
            xcopy(s, 0).wait_send()
            xcopy(s, 1).wait_recv()

        @pl.when(sx < rows - 1)
        def _():
            xcopy(s, 1).wait_send()
            xcopy(s, 0).wait_recv()

        stencil(s, lax.rem(s + 1, 3))

    def store(f):
        return pltpu.make_async_copy(
            q.at[0, f, pl.ds(2, X), pl.ds(8, Z), :], out.at[f], out_sem.at[f])

    @pl.loop(0, 5)
    def _(f):
        land(2, f, 0)
        store(f).start()

    @pl.loop(0, 5)
    def _(f):
        store(f).wait()

        @pl.loop(1, spans)
        def _(k):
            tile_copy(2, f, lax.rem(me + k, spans), me).wait_send()

    for k in range(1, spans):
        target_copy(lax.rem(me + k, spans), me).wait_send()


def body(rows, spans, perturbation, base_flow, donor_stream, donor_span, donor_weights,
         donor_receiver, target_stream, target_span):
    _, X, Z, Y = perturbation.shape
    donors = donor_stream.shape[1]
    cap = donors // 4
    slots = spans * cap
    assert Y == 128 and 2 * cap == 128 and rows > 2
    source = donor_stream * Z + donor_span
    target = target_stream * Z + target_span
    zero = jnp.zeros_like(donor_weights[0])
    meta = jnp.concatenate(
        [donor_receiver.astype(F32), source.astype(F32), donor_weights[0], donor_weights[1],
         donor_weights[2], target.astype(F32), zero, zero], axis=0)
    dma = pltpu.SemaphoreType.DMA
    return pl.pallas_call(
        functools.partial(kernel, rows, spans, X, Z, donors, cap),
        out_shape=jax.ShapeDtypeStruct(perturbation.shape, F32),
        in_specs=[pl.BlockSpec(memory_space=pl.ANY), pl.BlockSpec(memory_space=pl.ANY),
                  pl.BlockSpec(memory_space=pltpu.VMEM)],
        out_specs=pl.BlockSpec(memory_space=pl.ANY),
        scratch_shapes=[
            pltpu.VMEM((3, 5, X + 4, Z + 16, Y), F32),
            pltpu.VMEM((4, X, Z, Y), F32),
            pltpu.VMEM((5, spans, cap, Y), F32),
            pltpu.VMEM((3, 5, spans, cap, Y), F32),
            pltpu.VMEM((2, 5 * X * 2, Y), F32),
            pltpu.VMEM((3, 2, 5 * X * 2, Y), F32),
            pltpu.VMEM((spans, 8, 128), F32),
            pltpu.VMEM((spans, 8, 128), F32),
            pltpu.VMEM((slots, X * Z), BF16),
            pltpu.VMEM((slots, X * Z), BF16),
            pltpu.VMEM((slots, Y), F32),
            pltpu.VMEM(((X - 8) * Z, slots), BF16),
            pltpu.VMEM((X, Z, Y), F32),
            pltpu.VMEM((8, slots), F32),
            pltpu.VMEM((X * Z, 2 * Y), BF16),
            pltpu.VMEM((2 * Y, 2 * Y), BF16),
            pltpu.VMEM((5, Z, 2 * Y), F32),
            dma((6,)), dma((5,)), dma((5, spans)), dma((3, 5, spans)),
            dma((2,)), dma((3, 2)), dma((2,)), dma((3, 2)), dma((spans,)), dma((spans,)),
        ],
        compiler_params=pltpu.CompilerParams(
            collective_id=0, has_side_effects=True, vmem_limit_bytes=63 * 2**20),
    )(perturbation, base_flow, meta)


def solution(mesh):
    in_specs = (
        P(None, "stream", "span", None),
        P(None, "stream", "span", None),
        P("stream", "span"),
        P("stream", "span"),
        P(None, "stream", "span"),
        P("stream", "span"),
        P("stream", "span"),
        P("stream", "span"),
    )
    out_specs = P(None, "stream", "span", None)
    part = functools.partial(body, mesh.shape["stream"], mesh.shape["span"])
    return jax.shard_map(part, mesh=mesh, in_specs=in_specs, out_specs=out_specs, check_vma=False)
```

```python
import functools

import jax
import jax.numpy as jnp
from jax import lax
from jax.experimental import pallas as pl
from jax.experimental.pallas import tpu as pltpu
from jax.sharding import PartitionSpec as P

viscosity = 0.02
penalty_rate = 1.5
time_step = 0.25
MESH = pl.DeviceIdType.MESH
F32 = jnp.float32
BF16 = jnp.bfloat16


def split(values):
    high = values.astype(BF16)
    low = (values - high.astype(F32)).astype(BF16)
    return high, low


def kernel(
    rows, spans, X, Z, donors, cap,
    pert, flow_in, d_stream, d_span, d_weights, d_receiver, t_stream, t_span, out,
    q, flow, send, recv, zsend, zrecv, tsend, trecv,
    a_high, a_low, wy, landing, counted, trow, qcat, band, ybuf,
    load_sem, out_sem, send_sem, recv_sem, xs_sem, xr_sem, zs_sem, zr_sem, ts_sem, tr_sem,
):
    sx = lax.axis_index("stream")
    me = lax.axis_index("span")
    Y = 128
    slots = spans * cap

    def load(f):
        return pltpu.make_async_copy(
            pert.at[f], q.at[0, f, pl.ds(2, X), pl.ds(8, Z), :], load_sem.at[f])

    flow_load = pltpu.make_async_copy(flow_in, flow, load_sem.at[5])
    for f in range(5):
        load(f).start()
    flow_load.start()

    barrier = pltpu.get_barrier_semaphore()
    for k in range(1, spans):
        pl.semaphore_signal(barrier, inc=1, device_id=(sx, lax.rem(me + k, spans)), device_id_type=MESH)

    for k in (1, rows - 1):
        pl.semaphore_signal(barrier, inc=1, device_id=(lax.rem(sx + k, rows), me), device_id_type=MESH)
    pl.semaphore_wait(barrier, spans + 1)

    @pl.when(sx == 0)
    def _():
        for s in range(3):
            for f in range(5):
                q[s, f, 0:2, 8:8 + Z, :] = jnp.zeros((2, Z, Y), F32)

    @pl.when(sx == rows - 1)
    def _():
        for s in range(3):
            for f in range(5):
                q[s, f, X + 2:X + 4, 8:8 + Z, :] = jnp.zeros((2, Z, Y), F32)

    r = lax.broadcasted_iota(jnp.int32, (2 * Y, Y), 0) % Y
    c = lax.broadcasted_iota(jnp.int32, (2 * Y, Y), 1)
    gap = r - c
    near = jnp.abs(gap) == 1
    far = jnp.abs(gap) == 2
    band[:, 0:Y] = jnp.where(gap == 0, -30.0, jnp.where(near, 16.0, jnp.where(far, -1.0, 0.0))).astype(BF16)
    sign = jnp.where(gap > 0, 1.0, -1.0)
    band[:, Y:2 * Y] = (jnp.where(near, 8.0, jnp.where(far, -1.0, 0.0)) * sign).astype(BF16)

    dest_row = d_receiver[...].astype(F32)
    source_row = (d_stream[...] * Z + d_span[...]).astype(F32)
    fx_row = d_weights[0]
    fz_row = d_weights[1]
    fy_row = d_weights[2]
    target_row = (t_stream[...] * Z + t_span[...]).astype(F32)
    e_col = lax.broadcasted_iota(jnp.int32, (donors, donors), 0)
    e_row = lax.broadcasted_iota(jnp.int32, (donors, donors), 1)

    def to_col(row):
        return jnp.sum(jnp.where(e_col == e_row, row, 0.0), axis=1, keepdims=True)

    dest_col = to_col(dest_row)
    target_col = to_col(target_row)
    same = dest_col == dest_row
    rank_row = jnp.sum(jnp.where(same & (e_col < e_row), 1.0, 0.0), axis=0, keepdims=True)
    rank_col = jnp.sum(jnp.where(same & (e_row < e_col), 1.0, 0.0), axis=1, keepdims=True)
    position_row = dest_row * cap + rank_row
    lane = (lax.broadcasted_iota(jnp.int32, (donors, 128), 1) % cap).astype(F32)
    here = rank_col == lane
    for d in range(spans):
        picked = here & (dest_col == float(d))
        row = jnp.sum(jnp.where(picked, target_col + 1.0, 0.0), axis=0, keepdims=True) - 1.0
        tsend[d] = jnp.broadcast_to(row, (8, 128))

    def target_copy(peer, slot):
        return pltpu.make_async_remote_copy(
            src_ref=tsend.at[peer], dst_ref=trecv.at[slot], send_sem=ts_sem.at[peer],
            recv_sem=tr_sem.at[slot], device_id=(sx, peer), device_id_type=MESH)

    for k in range(1, spans):
        target_copy(lax.rem(me + k, spans), me).start()
    trecv[me] = tsend[me]

    for f in range(5):
        load(f).wait()

    def xcopy(s, side):
        first = 2 if side == 0 else X
        landed = X + 2 if side == 0 else 0
        peer = jnp.maximum(sx - 1, 0) if side == 0 else jnp.minimum(sx + 1, rows - 1)
        return pltpu.make_async_remote_copy(
            src_ref=q.at[s, :, pl.ds(first, 2), pl.ds(8, Z), :],
            dst_ref=q.at[s, :, pl.ds(landed, 2), pl.ds(8, Z), :],
            send_sem=xs_sem.at[side], recv_sem=xr_sem.at[s, side],
            device_id=(peer, me), device_id_type=MESH)

    def zcopy(s, side):
        peer = lax.rem(me + spans - 1, spans) if side == 0 else lax.rem(me + 1, spans)
        return pltpu.make_async_remote_copy(
            src_ref=zsend.at[side], dst_ref=zrecv.at[s, side],
            send_sem=zs_sem.at[side], recv_sem=zr_sem.at[s, side],
            device_id=(sx, peer), device_id_type=MESH)

    def send_halos(s):
        @pl.when(sx > 0)
        def _():
            xcopy(s, 0).start()

        @pl.when(sx < rows - 1)
        def _():
            xcopy(s, 1).start()

        for f in range(5):
            @pl.loop(0, X)
            def _(x):
                at = pl.ds((f * X + x) * 2, 2)
                zsend[0, at, :] = q[s, f, x + 2, 8:10, :]
                zsend[1, at, :] = q[s, f, x + 2, Z + 6:Z + 8, :]
        zcopy(s, 0).start()
        zcopy(s, 1).start()

    send_halos(0)

    @pl.loop(0, spans)
    def _(d):
        slot = (lax.broadcasted_iota(jnp.int32, (cap, donors), 0) + d * cap).astype(F32)
        mask = slot == position_row

        def pick(row):
            return jnp.sum(jnp.where(mask, row, 0.0), axis=1, keepdims=True)

        valid = pick(jnp.ones((1, donors), F32))
        source = pick(source_row).astype(jnp.int32)
        fx = pick(fx_row)
        fz = pick(fz_row)
        fy = pick(fy_row)
        wy[pl.ds(pl.multiple_of(d * cap, cap), cap), :] = jnp.broadcast_to(fy, (cap, Y))
        w00 = valid * (1.0 - fx) * (1.0 - fz)
        w10 = valid * fx * (1.0 - fz)
        w01 = valid * (1.0 - fx) * fz
        w11 = valid * fx * fz
        for j in range(X * Z // 256):
            col = lax.broadcasted_iota(jnp.int32, (cap, 256), 1) + j * 256 - source
            w = jnp.where(col == 0, w00, jnp.where(col == 1, w01, jnp.where(
                col == Z, w10, jnp.where(col == Z + 1, w11, 0.0))))
            high, low = split(w)
            a_high[pl.ds(pl.multiple_of(d * cap, cap), cap), j * 256:(j + 1) * 256] = high
            a_low[pl.ds(pl.multiple_of(d * cap, cap), cap), j * 256:(j + 1) * 256] = low

    def tile_copy(s, f, peer, slot):
        return pltpu.make_async_remote_copy(
            src_ref=send.at[f, peer], dst_ref=recv.at[s, f, slot],
            send_sem=send_sem.at[f, peer], recv_sem=recv_sem.at[s, f, slot],
            device_id=(sx, peer), device_id_type=MESH)

    def land(s, f, target):
        @pl.loop(1, spans)
        def _(k):
            tile_copy(s, f, lax.rem(me + k, spans), lax.rem(me + k, spans)).wait_recv()
        scale = penalty_rate * time_step * jnp.where(s == 0, 1.0, jnp.where(s == 1, 0.25, 2.0 / 3.0))
        high, low = split(recv[s, f].reshape(slots, Y))
        rhs = jnp.concatenate([high, low], axis=1)
        group = 8 if (X - 8) % 8 == 0 else 4

        @pl.loop(0, (X - 8) // group)
        def _(g):
            part = landing[pl.ds(pl.multiple_of(g * group * Z, group * Z), group * Z), :]
            both = jnp.dot(part, rhs, preferred_element_type=F32)
            total = (both[:, 0:Y] + both[:, Y:2 * Y]) * scale
            for i in range(group):
                x = 6 + g * group + i
                q[target, f, x, 8:8 + Z, :] = q[target, f, x, 8:8 + Z, :] + total[i * Z:(i + 1) * Z]

    def interpolate(s, f):
        @pl.loop(0, X)
        def _(x):
            high, low = split(q[s, f, 2 + x, 8:8 + Z, :])
            at = pl.ds(pl.multiple_of(x * Z, Z), Z)
            qcat[at, 0:Y] = high
            qcat[at, Y:2 * Y] = low

        @pl.when(s > 0)
        def _():
            @pl.loop(1, spans)
            def _(k):
                tile_copy(s, f, lax.rem(me + k, spans), me).wait_send()

        block = 256

        @pl.loop(0, slots // block)
        def _(g):
            at = pl.ds(pl.multiple_of(g * block, block), block)
            both = jnp.dot(a_high[at, :], qcat[...], preferred_element_type=F32)
            rest = jnp.dot(a_low[at, :], qcat[:, 0:Y], preferred_element_type=F32)
            value = both[:, 0:Y] + both[:, Y:2 * Y] + rest
            lane = lax.broadcasted_iota(jnp.int32, (block, Y), 1)
            shifted = jnp.where(lane == Y - 1, 0.0, pltpu.roll(value, Y - 1, 1))
            value = value + wy[at, :] * (shifted - value)
            for i in range(block // cap):
                send[f, g * (block // cap) + i] = value[i * cap:(i + 1) * cap]

        @pl.loop(1, spans)
        def _(k):
            tile_copy(s, f, lax.rem(me + k, spans), me).start()
        recv[s, f, me] = send[f, me]

    def build_landing():
        for k in range(1, spans):
            peer = lax.rem(me + k, spans)
            target_copy(peer, peer).wait_recv()
        lane = lax.broadcasted_iota(jnp.int32, (8, 128), 1)
        for p in range(spans // 2):
            trow[:, p * 128:(p + 1) * 128] = jnp.where(lane < cap, trecv[2 * p], trecv[2 * p + 1])

        @pl.loop(0, X)
        def _(x):
            counted[x] = jnp.zeros((Z, Y), F32)

        @pl.loop(4, X - 4)
        def _(x):
            col = (lax.broadcasted_iota(jnp.int32, (Z, slots), 0) + x * Z).astype(F32)
            hit = jnp.where(col == trow[0:1, :], 1.0, 0.0)
            landing[pl.ds(pl.multiple_of((x - 4) * Z, Z), Z), :] = hit.astype(BF16)
            counted[x] = jnp.broadcast_to(jnp.sum(hit, axis=1, keepdims=True), (Z, Y))

    def stencil(s, target):
        ours = jnp.where(s == 0, 0.0, jnp.where(s == 1, 0.75, 1.0 / 3.0))
        kept = jnp.where(s == 0, 1.0, jnp.where(s == 1, 0.25, 2.0 / 3.0))
        rate = kept * time_step
        twelfth = rate * (1.0 / 12.0)
        nu = viscosity * twelfth
        tall = 16

        @pl.loop(0, X)
        def _(x):
            pairs = []
            for f in range(5):
                pairs.append(jnp.concatenate(split(q[s, f, 2 + x, 8:8 + Z, :]), axis=1))
            wall = jnp.dot(jnp.concatenate(pairs, axis=0), band[...], preferred_element_type=F32)
            ybuf[...] = wall.reshape(5, Z, 2 * Y)

            @pl.loop(0, Z // tall)
            def _(t):
                z = t * tall
                zat = pl.ds(pl.multiple_of(z, tall), tall)
                stream_speed = flow[0, x, zat, :] * twelfth
                span_speed = flow[1, x, zat, :] * twelfth
                acoustic = flow[2, x, zat, :] * twelfth
                shear = flow[3, x, zat, :] * rate
                held = kept - (penalty_rate * rate) * counted[x, zat, :]
                result, dx, dz, mid = [], [], [], []
                for f in range(5):
                    def at(i, j):
                        return q[s, f, x + 2 + i, pl.ds(z + 8 + j, tall), :]
                    m = q[s, f, x + 2, pl.ds(pl.multiple_of(z + 8, 8), tall), :]
                    x0, x1, x3, x4 = at(-2, 0), at(-1, 0), at(1, 0), at(2, 0)
                    z0, z1, z3, z4 = at(0, -2), at(0, -1), at(0, 1), at(0, 2)
                    gx = 8.0 * (x3 - x1) - (x4 - x0)
                    gz = 8.0 * (z3 - z1) - (z4 - z0)
                    lap = 16.0 * ((x1 + x3) + (z1 + z3)) - ((x0 + x4) + (z0 + z4)) - 60.0 * m
                    lap = lap + ybuf[f, zat, 0:Y]
                    old = q[0, f, x + 2, pl.ds(pl.multiple_of(z + 8, 8), tall), :]
                    result.append(ours * old + held * m + nu * lap - stream_speed * gx - span_speed * gz)
                    dx.append(gx)
                    dz.append(gz)
                    mid.append(m)
                result[1] = result[1] - acoustic * dx[4] - shear * mid[2]
                result[2] = result[2] - acoustic * ybuf[4, zat, Y:2 * Y]
                result[3] = result[3] - acoustic * dz[4]
                result[4] = result[4] - acoustic * (dx[1] + ybuf[2, zat, Y:2 * Y] + dz[3])
                for f in range(5):
                    q[target, f, x + 2, pl.ds(pl.multiple_of(z + 8, 8), tall), :] = result[f]

    @pl.loop(0, 3)
    def _(s):
        @pl.loop(0, 5)
        def _(f):
            @pl.when(s > 0)
            def _():
                land(s - 1, f, s)
            interpolate(s, f)

        @pl.when(s == 0)
        def _():
            build_landing()
            flow_load.wait()

        zcopy(s, 0).wait()
        zcopy(s, 1).wait()
        for f in range(5):
            @pl.loop(0, X)
            def _(x):
                at = pl.ds((f * X + x) * 2, 2)
                q[s, f, x + 2, Z + 8:Z + 10, :] = zrecv[s, 0, at, :]
                q[s, f, x + 2, 6:8, :] = zrecv[s, 1, at, :]

        @pl.when(sx > 0)
        def _():
            xcopy(s, 0).wait_send()
            xcopy(s, 1).wait_recv()

        @pl.when(sx < rows - 1)
        def _():
            xcopy(s, 1).wait_send()
            xcopy(s, 0).wait_recv()

        stencil(s, lax.rem(s + 1, 3))

        @pl.when(s < 2)
        def _():
            send_halos(s + 1)

    def store(f):
        return pltpu.make_async_copy(
            q.at[0, f, pl.ds(2, X), pl.ds(8, Z), :], out.at[f], out_sem.at[f])

    @pl.loop(0, 5)
    def _(f):
        land(2, f, 0)
        store(f).start()

    @pl.loop(0, 5)
    def _(f):
        store(f).wait()

        @pl.loop(1, spans)
        def _(k):
            tile_copy(2, f, lax.rem(me + k, spans), me).wait_send()

    for k in range(1, spans):
        target_copy(lax.rem(me + k, spans), me).wait_send()


def body(rows, spans, perturbation, base_flow, donor_stream, donor_span, donor_weights,
         donor_receiver, target_stream, target_span):
    _, X, Z, Y = perturbation.shape
    donors = donor_stream.shape[1]
    cap = donors // 4
    slots = spans * cap
    assert Y == 128 and 2 * cap == 128 and rows > 2
    dma = pltpu.SemaphoreType.DMA
    return pl.pallas_call(
        functools.partial(kernel, rows, spans, X, Z, donors, cap),
        out_shape=jax.ShapeDtypeStruct(perturbation.shape, F32),
        in_specs=[pl.BlockSpec(memory_space=pl.ANY), pl.BlockSpec(memory_space=pl.ANY),
                  *[pl.BlockSpec(memory_space=pltpu.VMEM)] * 6],
        out_specs=pl.BlockSpec(memory_space=pl.ANY),
        scratch_shapes=[
            pltpu.VMEM((3, 5, X + 4, Z + 16, Y), F32),
            pltpu.VMEM((4, X, Z, Y), F32),
            pltpu.VMEM((5, spans, cap, Y), F32),
            pltpu.VMEM((3, 5, spans, cap, Y), F32),
            pltpu.VMEM((2, 5 * X * 2, Y), F32),
            pltpu.VMEM((3, 2, 5 * X * 2, Y), F32),
            pltpu.VMEM((spans, 8, 128), F32),
            pltpu.VMEM((spans, 8, 128), F32),
            pltpu.VMEM((slots, X * Z), BF16),
            pltpu.VMEM((slots, X * Z), BF16),
            pltpu.VMEM((slots, Y), F32),
            pltpu.VMEM(((X - 8) * Z, slots), BF16),
            pltpu.VMEM((X, Z, Y), F32),
            pltpu.VMEM((8, slots), F32),
            pltpu.VMEM((X * Z, 2 * Y), BF16),
            pltpu.VMEM((2 * Y, 2 * Y), BF16),
            pltpu.VMEM((5, Z, 2 * Y), F32),
            dma((6,)), dma((5,)), dma((5, spans)), dma((3, 5, spans)),
            dma((2,)), dma((3, 2)), dma((2,)), dma((3, 2)), dma((spans,)), dma((spans,)),
        ],
        compiler_params=pltpu.CompilerParams(
            collective_id=0, has_side_effects=True, vmem_limit_bytes=63 * 2**20),
    )(perturbation, base_flow, donor_stream, donor_span, donor_weights, donor_receiver,
      target_stream, target_span)


def solution(mesh):
    in_specs = (
        P(None, "stream", "span", None),
        P(None, "stream", "span", None),
        P("stream", "span"),
        P("stream", "span"),
        P(None, "stream", "span"),
        P("stream", "span"),
        P("stream", "span"),
        P("stream", "span"),
    )
    out_specs = P(None, "stream", "span", None)
    part = functools.partial(body, mesh.shape["stream"], mesh.shape["span"])
    return jax.shard_map(part, mesh=mesh, in_specs=in_specs, out_specs=out_specs, check_vma=False)
```

```python
import functools

import jax
import jax.numpy as jnp
from jax import lax
from jax.experimental import pallas as pl
from jax.experimental.pallas import tpu as pltpu
from jax.sharding import PartitionSpec as P

viscosity = 0.02
penalty_rate = 1.5
time_step = 0.25
MESH = pl.DeviceIdType.MESH
F32 = jnp.float32
BF16 = jnp.bfloat16


def split(values):
    high = values.astype(BF16)
    low = (values - high.astype(F32)).astype(BF16)
    return high, low


def kernel(
    rows, spans, X, Z, donors, cap,
    pert, flow_in, d_stream, d_span, d_weights, d_receiver, t_stream, t_span, out,
    q, flow, send, recv, zsend, zrecv, tsend, trecv,
    donor, wy, landing, counted, trow, qcat, band, ybuf,
    load_sem, out_sem, send_sem, recv_sem, xs_sem, xr_sem, zs_sem, zr_sem, ts_sem, tr_sem,
):
    sx = lax.axis_index("stream")
    me = lax.axis_index("span")
    Y = 128
    slots = spans * cap
    block = 256
    step = 4

    def load(f):
        return pltpu.make_async_copy(
            pert.at[f], q.at[0, f, pl.ds(2, X), pl.ds(8, Z), :], load_sem.at[f])

    flow_load = pltpu.make_async_copy(flow_in, flow, load_sem.at[5])
    for f in range(5):
        load(f).start()
    flow_load.start()

    barrier = pltpu.get_barrier_semaphore()
    for k in range(1, spans):
        pl.semaphore_signal(barrier, inc=1, device_id=(sx, lax.rem(me + k, spans)), device_id_type=MESH)

    for k in (1, rows - 1):
        pl.semaphore_signal(barrier, inc=1, device_id=(lax.rem(sx + k, rows), me), device_id_type=MESH)
    pl.semaphore_wait(barrier, spans + 1)

    @pl.when(sx == 0)
    def _():
        for s in range(3):
            for f in range(5):
                q[s, f, 0:2, 8:8 + Z, :] = jnp.zeros((2, Z, Y), F32)

    @pl.when(sx == rows - 1)
    def _():
        for s in range(3):
            for f in range(5):
                q[s, f, X + 2:X + 4, 8:8 + Z, :] = jnp.zeros((2, Z, Y), F32)

    r = lax.broadcasted_iota(jnp.int32, (2 * Y, Y), 0) % Y
    c = lax.broadcasted_iota(jnp.int32, (2 * Y, Y), 1)
    gap = r - c
    near = jnp.abs(gap) == 1
    far = jnp.abs(gap) == 2
    band[:, 0:Y] = jnp.where(gap == 0, -30.0, jnp.where(near, 16.0, jnp.where(far, -1.0, 0.0))).astype(BF16)
    sign = jnp.where(gap > 0, 1.0, -1.0)
    band[:, Y:2 * Y] = (jnp.where(near, 8.0, jnp.where(far, -1.0, 0.0)) * sign).astype(BF16)

    dest_row = d_receiver[...].astype(F32)
    source_row = (d_stream[...] * Z + d_span[...]).astype(F32)
    fx_row = d_weights[0]
    fz_row = d_weights[1]
    fy_row = d_weights[2]
    target_row = (t_stream[...] * Z + t_span[...]).astype(F32)
    e_col = lax.broadcasted_iota(jnp.int32, (donors, donors), 0)
    e_row = lax.broadcasted_iota(jnp.int32, (donors, donors), 1)

    def to_col(row):
        return jnp.sum(jnp.where(e_col == e_row, row, 0.0), axis=1, keepdims=True)

    dest_col = to_col(dest_row)
    target_col = to_col(target_row)
    same = dest_col == dest_row
    rank_row = jnp.sum(jnp.where(same & (e_col < e_row), 1.0, 0.0), axis=0, keepdims=True)
    rank_col = jnp.sum(jnp.where(same & (e_row < e_col), 1.0, 0.0), axis=1, keepdims=True)
    position_row = dest_row * cap + rank_row
    lane = (lax.broadcasted_iota(jnp.int32, (donors, 128), 1) % cap).astype(F32)
    here = rank_col == lane
    for d in range(spans):
        picked = here & (dest_col == float(d))
        row = jnp.sum(jnp.where(picked, target_col + 1.0, 0.0), axis=0, keepdims=True) - 1.0
        tsend[d] = jnp.broadcast_to(row, (8, 128))

    def target_copy(peer, slot):
        return pltpu.make_async_remote_copy(
            src_ref=tsend.at[peer], dst_ref=trecv.at[slot], send_sem=ts_sem.at[peer],
            recv_sem=tr_sem.at[slot], device_id=(sx, peer), device_id_type=MESH)

    for k in range(1, spans):
        target_copy(lax.rem(me + k, spans), me).start()
    trecv[me] = tsend[me]

    for f in range(5):
        load(f).wait()

    def xcopy(s, side):
        first = 2 if side == 0 else X
        landed = X + 2 if side == 0 else 0
        peer = jnp.maximum(sx - 1, 0) if side == 0 else jnp.minimum(sx + 1, rows - 1)
        return pltpu.make_async_remote_copy(
            src_ref=q.at[s, :, pl.ds(first, 2), pl.ds(8, Z), :],
            dst_ref=q.at[s, :, pl.ds(landed, 2), pl.ds(8, Z), :],
            send_sem=xs_sem.at[side], recv_sem=xr_sem.at[s, side],
            device_id=(peer, me), device_id_type=MESH)

    def zcopy(s, side):
        peer = lax.rem(me + spans - 1, spans) if side == 0 else lax.rem(me + 1, spans)
        return pltpu.make_async_remote_copy(
            src_ref=zsend.at[side], dst_ref=zrecv.at[s, side],
            send_sem=zs_sem.at[side], recv_sem=zr_sem.at[s, side],
            device_id=(sx, peer), device_id_type=MESH)

    def send_halos(s):
        @pl.when(sx > 0)
        def _():
            xcopy(s, 0).start()

        @pl.when(sx < rows - 1)
        def _():
            xcopy(s, 1).start()

        @pl.loop(0, X // step)
        def _(xo):
            for f in range(5):
                for i in range(step):
                    x = xo * step + i
                    at = pl.ds((f * X + x) * 2, 2)
                    zsend[0, at, :] = q[s, f, x + 2, 8:10, :]
                    zsend[1, at, :] = q[s, f, x + 2, Z + 6:Z + 8, :]
        zcopy(s, 0).start()
        zcopy(s, 1).start()

    send_halos(0)

    @pl.loop(0, spans)
    def _(d):
        slot = (lax.broadcasted_iota(jnp.int32, (cap, donors), 0) + d * cap).astype(F32)
        mask = slot == position_row
        first = (d // (block // cap)) * (2 * block) + (d % (block // cap)) * cap

        def pick(row):
            return jnp.sum(jnp.where(mask, row, 0.0), axis=1, keepdims=True)

        valid = pick(jnp.ones((1, donors), F32))
        source = pick(source_row).astype(jnp.int32)
        fx = pick(fx_row)
        fz = pick(fz_row)
        fy = pick(fy_row)
        wy[pl.ds(pl.multiple_of(d * cap, cap), cap), :] = jnp.broadcast_to(fy, (cap, Y))
        w00 = valid * (1.0 - fx) * (1.0 - fz)
        w10 = valid * fx * (1.0 - fz)
        w01 = valid * (1.0 - fx) * fz
        w11 = valid * fx * fz
        for j in range(X * Z // 256):
            col = lax.broadcasted_iota(jnp.int32, (cap, 256), 1) + j * 256 - source
            w = jnp.where(col == 0, w00, jnp.where(col == 1, w01, jnp.where(
                col == Z, w10, jnp.where(col == Z + 1, w11, 0.0))))
            high, low = split(w)
            donor[pl.ds(pl.multiple_of(first, cap), cap), j * 256:(j + 1) * 256] = high
            donor[pl.ds(pl.multiple_of(first + block, cap), cap), j * 256:(j + 1) * 256] = low

    def tile_copy(s, f, peer, slot):
        return pltpu.make_async_remote_copy(
            src_ref=send.at[f, peer], dst_ref=recv.at[s, f, slot],
            send_sem=send_sem.at[f, peer], recv_sem=recv_sem.at[s, f, slot],
            device_id=(sx, peer), device_id_type=MESH)

    def land(s, f, target):
        @pl.loop(1, spans)
        def _(k):
            tile_copy(s, f, lax.rem(me + k, spans), lax.rem(me + k, spans)).wait_recv()
        scale = penalty_rate * time_step * jnp.where(s == 0, 1.0, jnp.where(s == 1, 0.25, 2.0 / 3.0))
        high, low = split(recv[s, f].reshape(slots, Y))
        rhs = jnp.concatenate([high, low], axis=1)
        group = 8 if (X - 8) % 8 == 0 else 4

        @pl.loop(0, (X - 8) // group)
        def _(g):
            part = landing[pl.ds(pl.multiple_of(g * group * Z, group * Z), group * Z), :]
            both = jnp.dot(part, rhs, preferred_element_type=F32)
            total = (both[:, 0:Y] + both[:, Y:2 * Y]) * scale
            for i in range(group):
                x = 6 + g * group + i
                q[target, f, x, 8:8 + Z, :] = q[target, f, x, 8:8 + Z, :] + total[i * Z:(i + 1) * Z]

    def interpolate(s, f):
        @pl.loop(0, X // step)
        def _(xo):
            for i in range(step):
                x = xo * step + i
                high, low = split(q[s, f, 2 + x, 8:8 + Z, :])
                at = pl.ds(pl.multiple_of(x * Z, Z), Z)
                qcat[at, 0:Y] = high
                qcat[at, Y:2 * Y] = low

        @pl.when(s > 0)
        def _():
            @pl.loop(1, spans)
            def _(k):
                tile_copy(s, f, lax.rem(me + k, spans), me).wait_send()

        @pl.loop(0, slots // block)
        def _(g):
            at = pl.ds(pl.multiple_of(g * block, block), block)
            pair = pl.ds(pl.multiple_of(g * (2 * block), 2 * block), 2 * block)
            both = jnp.dot(donor[pair, :], qcat[...], preferred_element_type=F32)
            value = both[0:block, 0:Y] + both[0:block, Y:2 * Y] + both[block:2 * block, 0:Y]
            lane = lax.broadcasted_iota(jnp.int32, (block, Y), 1)
            shifted = jnp.where(lane == Y - 1, 0.0, pltpu.roll(value, Y - 1, 1))
            value = value + wy[at, :] * (shifted - value)
            for i in range(block // cap):
                send[f, g * (block // cap) + i] = value[i * cap:(i + 1) * cap]

        @pl.loop(1, spans)
        def _(k):
            tile_copy(s, f, lax.rem(me + k, spans), me).start()
        recv[s, f, me] = send[f, me]

    def build_landing():
        for k in range(1, spans):
            peer = lax.rem(me + k, spans)
            target_copy(peer, peer).wait_recv()
        lane = lax.broadcasted_iota(jnp.int32, (8, 128), 1)
        for p in range(spans // 2):
            trow[:, p * 128:(p + 1) * 128] = jnp.where(lane < cap, trecv[2 * p], trecv[2 * p + 1])

        @pl.loop(0, X)
        def _(x):
            counted[x] = jnp.zeros((Z, Y), F32)

        @pl.loop(4, X - 4)
        def _(x):
            col = (lax.broadcasted_iota(jnp.int32, (Z, slots), 0) + x * Z).astype(F32)
            hit = jnp.where(col == trow[0:1, :], 1.0, 0.0)
            landing[pl.ds(pl.multiple_of((x - 4) * Z, Z), Z), :] = hit.astype(BF16)
            counted[x] = jnp.broadcast_to(jnp.sum(hit, axis=1, keepdims=True), (Z, Y))

    def stencil(s, target):
        ours = jnp.where(s == 0, 0.0, jnp.where(s == 1, 0.75, 1.0 / 3.0))
        kept = jnp.where(s == 0, 1.0, jnp.where(s == 1, 0.25, 2.0 / 3.0))
        rate = kept * time_step
        twelfth = rate * (1.0 / 12.0)
        nu = viscosity * twelfth
        tall = 16

        @pl.loop(0, X // step)
        def _(xo):
            for i in range(step):
                pairs = []
                for f in range(5):
                    pairs.append(jnp.concatenate(split(q[s, f, 2 + xo * step + i, 8:8 + Z, :]), axis=1))
                wall = jnp.dot(jnp.concatenate(pairs, axis=0), band[...], preferred_element_type=F32)
                ybuf[i] = wall.reshape(5, Z, 2 * Y)

            @pl.loop(0, step * (Z // tall))
            def _(t):
                row = t // (Z // tall)
                x = xo * step + row
                z = (t % (Z // tall)) * tall
                zat = pl.ds(pl.multiple_of(z, tall), tall)
                stream_speed = flow[0, x, zat, :] * twelfth
                span_speed = flow[1, x, zat, :] * twelfth
                acoustic = flow[2, x, zat, :] * twelfth
                shear = flow[3, x, zat, :] * rate
                held = kept - (penalty_rate * rate) * counted[x, zat, :]
                result, dx, dz, mid = [], [], [], []
                for f in range(5):
                    def at(i, j):
                        return q[s, f, x + 2 + i, pl.ds(z + 8 + j, tall), :]
                    m = q[s, f, x + 2, pl.ds(pl.multiple_of(z + 8, 8), tall), :]
                    x0, x1, x3, x4 = at(-2, 0), at(-1, 0), at(1, 0), at(2, 0)
                    z0, z1, z3, z4 = at(0, -2), at(0, -1), at(0, 1), at(0, 2)
                    gx = 8.0 * (x3 - x1) - (x4 - x0)
                    gz = 8.0 * (z3 - z1) - (z4 - z0)
                    lap = 16.0 * ((x1 + x3) + (z1 + z3)) - ((x0 + x4) + (z0 + z4)) - 60.0 * m
                    lap = lap + ybuf[row, f, zat, 0:Y]
                    old = q[0, f, x + 2, pl.ds(pl.multiple_of(z + 8, 8), tall), :]
                    result.append(ours * old + held * m + nu * lap - stream_speed * gx - span_speed * gz)
                    dx.append(gx)
                    dz.append(gz)
                    mid.append(m)
                result[1] = result[1] - acoustic * dx[4] - shear * mid[2]
                result[2] = result[2] - acoustic * ybuf[row, 4, zat, Y:2 * Y]
                result[3] = result[3] - acoustic * dz[4]
                result[4] = result[4] - acoustic * (dx[1] + ybuf[row, 2, zat, Y:2 * Y] + dz[3])
                for f in range(5):
                    q[target, f, x + 2, pl.ds(pl.multiple_of(z + 8, 8), tall), :] = result[f]

    @pl.loop(0, 3)
    def _(s):
        @pl.loop(0, 5)
        def _(f):
            @pl.when(s > 0)
            def _():
                land(s - 1, f, s)
            interpolate(s, f)

        @pl.when(s == 0)
        def _():
            build_landing()
            flow_load.wait()

        zcopy(s, 0).wait()
        zcopy(s, 1).wait()
        @pl.loop(0, X // step)
        def _(xo):
            for f in range(5):
                for i in range(step):
                    x = xo * step + i
                    at = pl.ds((f * X + x) * 2, 2)
                    q[s, f, x + 2, Z + 8:Z + 10, :] = zrecv[s, 0, at, :]
                    q[s, f, x + 2, 6:8, :] = zrecv[s, 1, at, :]

        @pl.when(sx > 0)
        def _():
            xcopy(s, 0).wait_send()
            xcopy(s, 1).wait_recv()

        @pl.when(sx < rows - 1)
        def _():
            xcopy(s, 1).wait_send()
            xcopy(s, 0).wait_recv()

        stencil(s, lax.rem(s + 1, 3))

        @pl.when(s < 2)
        def _():
            send_halos(s + 1)

    def store(f):
        return pltpu.make_async_copy(
            q.at[0, f, pl.ds(2, X), pl.ds(8, Z), :], out.at[f], out_sem.at[f])

    @pl.loop(0, 5)
    def _(f):
        land(2, f, 0)
        store(f).start()

    @pl.loop(0, 5)
    def _(f):
        store(f).wait()

        @pl.loop(1, spans)
        def _(k):
            tile_copy(2, f, lax.rem(me + k, spans), me).wait_send()

    for k in range(1, spans):
        target_copy(lax.rem(me + k, spans), me).wait_send()


def body(rows, spans, perturbation, base_flow, donor_stream, donor_span, donor_weights,
         donor_receiver, target_stream, target_span):
    _, X, Z, Y = perturbation.shape
    donors = donor_stream.shape[1]
    cap = donors // 4
    slots = spans * cap
    assert Y == 128 and 2 * cap == 128 and rows > 2 and X % 4 == 0
    dma = pltpu.SemaphoreType.DMA
    return pl.pallas_call(
        functools.partial(kernel, rows, spans, X, Z, donors, cap),
        out_shape=jax.ShapeDtypeStruct(perturbation.shape, F32),
        in_specs=[pl.BlockSpec(memory_space=pl.ANY), pl.BlockSpec(memory_space=pl.ANY),
                  *[pl.BlockSpec(memory_space=pltpu.VMEM)] * 6],
        out_specs=pl.BlockSpec(memory_space=pl.ANY),
        scratch_shapes=[
            pltpu.VMEM((3, 5, X + 4, Z + 16, Y), F32),
            pltpu.VMEM((4, X, Z, Y), F32),
            pltpu.VMEM((5, spans, cap, Y), F32),
            pltpu.VMEM((3, 5, spans, cap, Y), F32),
            pltpu.VMEM((2, 5 * X * 2, Y), F32),
            pltpu.VMEM((3, 2, 5 * X * 2, Y), F32),
            pltpu.VMEM((spans, 8, 128), F32),
            pltpu.VMEM((spans, 8, 128), F32),
            pltpu.VMEM((2 * slots, X * Z), BF16),
            pltpu.VMEM((slots, Y), F32),
            pltpu.VMEM(((X - 8) * Z, slots), BF16),
            pltpu.VMEM((X, Z, Y), F32),
            pltpu.VMEM((8, slots), F32),
            pltpu.VMEM((X * Z, 2 * Y), BF16),
            pltpu.VMEM((2 * Y, 2 * Y), BF16),
            pltpu.VMEM((4, 5, Z, 2 * Y), F32),
            dma((6,)), dma((5,)), dma((5, spans)), dma((3, 5, spans)),
            dma((2,)), dma((3, 2)), dma((2,)), dma((3, 2)), dma((spans,)), dma((spans,)),
        ],
        compiler_params=pltpu.CompilerParams(
            collective_id=0, has_side_effects=True, vmem_limit_bytes=63 * 2**20),
    )(perturbation, base_flow, donor_stream, donor_span, donor_weights, donor_receiver,
      target_stream, target_span)


def solution(mesh):
    in_specs = (
        P(None, "stream", "span", None),
        P(None, "stream", "span", None),
        P("stream", "span"),
        P("stream", "span"),
        P(None, "stream", "span"),
        P("stream", "span"),
        P("stream", "span"),
        P("stream", "span"),
    )
    out_specs = P(None, "stream", "span", None)
    part = functools.partial(body, mesh.shape["stream"], mesh.shape["span"])
    return jax.shard_map(part, mesh=mesh, in_specs=in_specs, out_specs=out_specs, check_vma=False)
```

```python
import functools

import jax
import jax.numpy as jnp
from jax import lax
from jax.experimental import pallas as pl
from jax.experimental.pallas import tpu as pltpu
from jax.sharding import PartitionSpec as P

viscosity = 0.02
penalty_rate = 1.5
time_step = 0.25
MESH = pl.DeviceIdType.MESH
F32 = jnp.float32
BF16 = jnp.bfloat16


def split(values):
    high = values.astype(BF16)
    low = (values - high.astype(F32)).astype(BF16)
    return high, low


def kernel(
    rows, spans, X, Z, donors, cap,
    pert, flow_in, d_stream, d_span, d_weights, d_receiver, t_stream, t_span, out,
    q, flow, send, recv, zsend, zrecv, tsend, trecv,
    donor, wy, landing, counted, trow, qcat, band, ybuf,
    load_sem, out_sem, send_sem, recv_sem, xs_sem, xr_sem, zs_sem, zr_sem, ts_sem, tr_sem,
):
    sx = lax.axis_index("stream")
    me = lax.axis_index("span")
    Y = 128
    slots = spans * cap
    block = 256
    step = 4

    def load(f):
        return pltpu.make_async_copy(
            pert.at[f], q.at[0, f, pl.ds(2, X), pl.ds(8, Z), :], load_sem.at[f])

    flow_load = pltpu.make_async_copy(flow_in, flow, load_sem.at[5])
    for f in range(5):
        load(f).start()
    flow_load.start()

    barrier = pltpu.get_barrier_semaphore()
    for k in range(1, spans):
        pl.semaphore_signal(barrier, inc=1, device_id=(sx, lax.rem(me + k, spans)), device_id_type=MESH)

    for k in (1, rows - 1):
        pl.semaphore_signal(barrier, inc=1, device_id=(lax.rem(sx + k, rows), me), device_id_type=MESH)
    pl.semaphore_wait(barrier, spans + 1)

    @pl.when(sx == 0)
    def _():
        for s in range(3):
            for f in range(5):
                q[s, f, 0:2, 8:8 + Z, :] = jnp.zeros((2, Z, Y), F32)

    @pl.when(sx == rows - 1)
    def _():
        for s in range(3):
            for f in range(5):
                q[s, f, X + 2:X + 4, 8:8 + Z, :] = jnp.zeros((2, Z, Y), F32)

    r = lax.broadcasted_iota(jnp.int32, (2 * Y, Y), 0) % Y
    c = lax.broadcasted_iota(jnp.int32, (2 * Y, Y), 1)
    gap = r - c
    near = jnp.abs(gap) == 1
    far = jnp.abs(gap) == 2
    band[:, 0:Y] = jnp.where(gap == 0, -30.0, jnp.where(near, 16.0, jnp.where(far, -1.0, 0.0))).astype(BF16)
    sign = jnp.where(gap > 0, 1.0, -1.0)
    band[:, Y:2 * Y] = (jnp.where(near, 8.0, jnp.where(far, -1.0, 0.0)) * sign).astype(BF16)

    dest_row = d_receiver[...].astype(F32)
    source_row = (d_stream[...] * Z + d_span[...]).astype(F32)
    fx_row = d_weights[0]
    fz_row = d_weights[1]
    fy_row = d_weights[2]
    target_row = (t_stream[...] * Z + t_span[...]).astype(F32)
    e_col = lax.broadcasted_iota(jnp.int32, (donors, donors), 0)
    e_row = lax.broadcasted_iota(jnp.int32, (donors, donors), 1)

    def to_col(row):
        return jnp.sum(jnp.where(e_col == e_row, row, 0.0), axis=1, keepdims=True)

    dest_col = to_col(dest_row)
    target_col = to_col(target_row)
    same = dest_col == dest_row
    rank_row = jnp.sum(jnp.where(same & (e_col < e_row), 1.0, 0.0), axis=0, keepdims=True)
    rank_col = jnp.sum(jnp.where(same & (e_row < e_col), 1.0, 0.0), axis=1, keepdims=True)
    position_row = dest_row * cap + rank_row
    lane = (lax.broadcasted_iota(jnp.int32, (donors, 128), 1) % cap).astype(F32)
    here = rank_col == lane
    for d in range(spans):
        picked = here & (dest_col == float(d))
        row = jnp.sum(jnp.where(picked, target_col + 1.0, 0.0), axis=0, keepdims=True) - 1.0
        tsend[d] = jnp.broadcast_to(row, (8, 128))

    def target_copy(peer, slot):
        return pltpu.make_async_remote_copy(
            src_ref=tsend.at[peer], dst_ref=trecv.at[slot], send_sem=ts_sem.at[peer],
            recv_sem=tr_sem.at[slot], device_id=(sx, peer), device_id_type=MESH)

    for k in range(1, spans):
        target_copy(lax.rem(me + k, spans), me).start()
    trecv[me] = tsend[me]

    for f in range(5):
        load(f).wait()

    def xcopy(s, side):
        first = 2 if side == 0 else X
        landed = X + 2 if side == 0 else 0
        peer = jnp.maximum(sx - 1, 0) if side == 0 else jnp.minimum(sx + 1, rows - 1)
        return pltpu.make_async_remote_copy(
            src_ref=q.at[s, :, pl.ds(first, 2), pl.ds(8, Z), :],
            dst_ref=q.at[s, :, pl.ds(landed, 2), pl.ds(8, Z), :],
            send_sem=xs_sem.at[side], recv_sem=xr_sem.at[s, side],
            device_id=(peer, me), device_id_type=MESH)

    def zcopy(s, side):
        peer = lax.rem(me + spans - 1, spans) if side == 0 else lax.rem(me + 1, spans)
        return pltpu.make_async_remote_copy(
            src_ref=zsend.at[side], dst_ref=zrecv.at[s, side],
            send_sem=zs_sem.at[side], recv_sem=zr_sem.at[s, side],
            device_id=(sx, peer), device_id_type=MESH)

    def send_halos(s):
        @pl.when(sx > 0)
        def _():
            xcopy(s, 0).start()

        @pl.when(sx < rows - 1)
        def _():
            xcopy(s, 1).start()

        @pl.loop(0, X // step)
        def _(xo):
            for f in range(5):
                for i in range(step):
                    x = xo * step + i
                    at = pl.ds((f * X + x) * 2, 2)
                    zsend[0, at, :] = q[s, f, x + 2, 8:10, :]
                    zsend[1, at, :] = q[s, f, x + 2, Z + 6:Z + 8, :]
        zcopy(s, 0).start()
        zcopy(s, 1).start()

    send_halos(0)

    @pl.loop(0, spans)
    def _(d):
        slot = (lax.broadcasted_iota(jnp.int32, (cap, donors), 0) + d * cap).astype(F32)
        mask = slot == position_row
        first = (d // (block // cap)) * (2 * block) + (d % (block // cap)) * cap

        def pick(row):
            return jnp.sum(jnp.where(mask, row, 0.0), axis=1, keepdims=True)

        valid = pick(jnp.ones((1, donors), F32))
        source = pick(source_row).astype(jnp.int32)
        fx = pick(fx_row)
        fz = pick(fz_row)
        fy = pick(fy_row)
        wy[pl.ds(pl.multiple_of(d * cap, cap), cap), :] = jnp.broadcast_to(fy, (cap, Y))
        w00 = valid * (1.0 - fx) * (1.0 - fz)
        w10 = valid * fx * (1.0 - fz)
        w01 = valid * (1.0 - fx) * fz
        w11 = valid * fx * fz
        for j in range(X * Z // 256):
            col = lax.broadcasted_iota(jnp.int32, (cap, 256), 1) + j * 256 - source
            w = jnp.where(col == 0, w00, jnp.where(col == 1, w01, jnp.where(
                col == Z, w10, jnp.where(col == Z + 1, w11, 0.0))))
            high, low = split(w)
            donor[pl.ds(pl.multiple_of(first, cap), cap), j * 256:(j + 1) * 256] = high
            donor[pl.ds(pl.multiple_of(first + block, cap), cap), j * 256:(j + 1) * 256] = low

    def tile_copy(s, f, peer, slot):
        return pltpu.make_async_remote_copy(
            src_ref=send.at[f, peer], dst_ref=recv.at[s, f, slot],
            send_sem=send_sem.at[f, peer], recv_sem=recv_sem.at[s, f, slot],
            device_id=(sx, peer), device_id_type=MESH)

    def land(s, f, target):
        @pl.loop(1, spans)
        def _(k):
            tile_copy(s, f, lax.rem(me + k, spans), lax.rem(me + k, spans)).wait_recv()
        scale = penalty_rate * time_step * jnp.where(s == 0, 1.0, jnp.where(s == 1, 0.25, 2.0 / 3.0))
        high, low = split(recv[s, f].reshape(slots, Y))
        rhs = jnp.concatenate([high, low], axis=1)
        group = 8 if (X - 8) % 8 == 0 else 4

        @pl.loop(0, (X - 8) // group)
        def _(g):
            part = landing[pl.ds(pl.multiple_of(g * group * Z, group * Z), group * Z), :]
            both = jnp.dot(part, rhs, preferred_element_type=F32)
            total = (both[:, 0:Y] + both[:, Y:2 * Y]) * scale
            for i in range(group):
                x = 6 + g * group + i
                q[target, f, x, 8:8 + Z, :] = q[target, f, x, 8:8 + Z, :] + total[i * Z:(i + 1) * Z]

    def interpolate(s, f):
        @pl.loop(0, X // step)
        def _(xo):
            for i in range(step):
                x = xo * step + i
                high, low = split(q[s, f, 2 + x, 8:8 + Z, :])
                at = pl.ds(pl.multiple_of(x * Z, Z), Z)
                qcat[at, 0:Y] = high
                qcat[at, Y:2 * Y] = low

        @pl.when(s > 0)
        def _():
            @pl.loop(1, spans)
            def _(k):
                tile_copy(s, f, lax.rem(me + k, spans), me).wait_send()

        @pl.loop(0, slots // block)
        def _(g):
            at = pl.ds(pl.multiple_of(g * block, block), block)
            pair = pl.ds(pl.multiple_of(g * (2 * block), 2 * block), 2 * block)
            both = jnp.dot(donor[pair, :], qcat[...], preferred_element_type=F32)
            value = both[0:block, 0:Y] + both[0:block, Y:2 * Y] + both[block:2 * block, 0:Y]
            lane = lax.broadcasted_iota(jnp.int32, (block, Y), 1)
            shifted = jnp.where(lane == Y - 1, 0.0, pltpu.roll(value, Y - 1, 1))
            value = value + wy[at, :] * (shifted - value)
            for i in range(block // cap):
                send[f, g * (block // cap) + i] = value[i * cap:(i + 1) * cap]

        @pl.loop(1, spans)
        def _(k):
            tile_copy(s, f, lax.rem(me + k, spans), me).start()
        recv[s, f, me] = send[f, me]

    def build_landing():
        for k in range(1, spans):
            peer = lax.rem(me + k, spans)
            target_copy(peer, peer).wait_recv()
        lane = lax.broadcasted_iota(jnp.int32, (8, 128), 1)
        for p in range(spans // 2):
            trow[:, p * 128:(p + 1) * 128] = jnp.where(lane < cap, trecv[2 * p], trecv[2 * p + 1])

        @pl.loop(0, X)
        def _(x):
            counted[x] = jnp.zeros((Z, Y), F32)

        @pl.loop(4, X - 4)
        def _(x):
            col = (lax.broadcasted_iota(jnp.int32, (Z, slots), 0) + x * Z).astype(F32)
            hit = jnp.where(col == trow[0:1, :], 1.0, 0.0)
            landing[pl.ds(pl.multiple_of((x - 4) * Z, Z), Z), :] = hit.astype(BF16)
            counted[x] = jnp.broadcast_to(jnp.sum(hit, axis=1, keepdims=True), (Z, Y))

    def stencil(s, target):
        ours = jnp.where(s == 0, 0.0, jnp.where(s == 1, 0.75, 1.0 / 3.0))
        kept = jnp.where(s == 0, 1.0, jnp.where(s == 1, 0.25, 2.0 / 3.0))
        rate = kept * time_step
        twelfth = rate * (1.0 / 12.0)
        nu = viscosity * twelfth
        tall = 16

        @pl.loop(0, X // step)
        def _(xo):
            for i in range(step):
                pairs = []
                for f in range(5):
                    pairs.append(jnp.concatenate(split(q[s, f, 2 + xo * step + i, 8:8 + Z, :]), axis=1))
                wall = jnp.dot(jnp.concatenate(pairs, axis=0), band[...], preferred_element_type=F32)
                ybuf[i] = wall.reshape(5, Z, 2 * Y)

            @pl.loop(0, step * (Z // tall))
            def _(t):
                row = t // (Z // tall)
                x = xo * step + row
                z = (t % (Z // tall)) * tall
                zat = pl.ds(pl.multiple_of(z, tall), tall)
                stream_speed = flow[0, x, zat, :] * twelfth
                span_speed = flow[1, x, zat, :] * twelfth
                acoustic = flow[2, x, zat, :] * twelfth
                shear = flow[3, x, zat, :] * rate
                held = kept - (penalty_rate * rate) * counted[x, zat, :]
                result, dx, dz, mid = [], [], [], []
                for f in range(5):
                    def at(i, j):
                        return q[s, f, x + 2 + i, pl.ds(z + 8 + j, tall), :]
                    m = q[s, f, x + 2, pl.ds(pl.multiple_of(z + 8, 8), tall), :]
                    x0, x1, x3, x4 = at(-2, 0), at(-1, 0), at(1, 0), at(2, 0)
                    z0, z1, z3, z4 = at(0, -2), at(0, -1), at(0, 1), at(0, 2)
                    gx = 8.0 * (x3 - x1) - (x4 - x0)
                    gz = 8.0 * (z3 - z1) - (z4 - z0)
                    lap = 16.0 * ((x1 + x3) + (z1 + z3)) - ((x0 + x4) + (z0 + z4)) - 60.0 * m
                    lap = lap + ybuf[row, f, zat, 0:Y]
                    old = q[0, f, x + 2, pl.ds(pl.multiple_of(z + 8, 8), tall), :]
                    result.append(ours * old + held * m + nu * lap - stream_speed * gx - span_speed * gz)
                    dx.append(gx)
                    dz.append(gz)
                    mid.append(m)
                result[1] = result[1] - acoustic * dx[4] - shear * mid[2]
                result[2] = result[2] - acoustic * ybuf[row, 4, zat, Y:2 * Y]
                result[3] = result[3] - acoustic * dz[4]
                result[4] = result[4] - acoustic * (dx[1] + ybuf[row, 2, zat, Y:2 * Y] + dz[3])
                for f in range(5):
                    q[target, f, x + 2, pl.ds(pl.multiple_of(z + 8, 8), tall), :] = result[f]

    @pl.loop(0, 3)
    def _(s):
        @pl.loop(0, 5)
        def _(f):
            @pl.when(s > 0)
            def _():
                land(s - 1, f, s)
            interpolate(s, f)

        @pl.when(s == 0)
        def _():
            build_landing()
            flow_load.wait()

        zcopy(s, 0).wait()
        zcopy(s, 1).wait()
        @pl.loop(0, X // step)
        def _(xo):
            for f in range(5):
                for i in range(step):
                    x = xo * step + i
                    at = pl.ds((f * X + x) * 2, 2)
                    q[s, f, x + 2, Z + 8:Z + 10, :] = zrecv[s, 0, at, :]
                    q[s, f, x + 2, 6:8, :] = zrecv[s, 1, at, :]

        @pl.when(sx > 0)
        def _():
            xcopy(s, 0).wait_send()
            xcopy(s, 1).wait_recv()

        @pl.when(sx < rows - 1)
        def _():
            xcopy(s, 1).wait_send()
            xcopy(s, 0).wait_recv()

        stencil(s, lax.rem(s + 1, 3))

        @pl.when(s < 2)
        def _():
            send_halos(s + 1)

    def store(f):
        return pltpu.make_async_copy(
            q.at[0, f, pl.ds(2, X), pl.ds(8, Z), :], out.at[f], out_sem.at[f])

    @pl.loop(0, 5)
    def _(f):
        land(2, f, 0)
        store(f).start()

    @pl.loop(0, 5)
    def _(f):
        store(f).wait()

        @pl.loop(1, spans)
        def _(k):
            tile_copy(2, f, lax.rem(me + k, spans), me).wait_send()

    for k in range(1, spans):
        target_copy(lax.rem(me + k, spans), me).wait_send()


def deliver(state, out, held, in_sem, out_sem):
    parts, half = 2, state.shape[1] // 2

    def pieces(ref, k):
        return ref.at[k // parts, pl.ds((k % parts) * half, half)]

    total = state.shape[0] * parts
    for k in range(total):
        pltpu.make_async_copy(pieces(state, k), pieces(held, k), in_sem.at[k]).start()
    for k in range(total):
        pltpu.make_async_copy(pieces(state, k), pieces(held, k), in_sem.at[k]).wait()
        pltpu.make_async_copy(pieces(held, k), pieces(out, k), out_sem.at[k]).start()
    for k in range(total):
        pltpu.make_async_copy(pieces(held, k), pieces(out, k), out_sem.at[k]).wait()


def body(rows, spans, perturbation, base_flow, donor_stream, donor_span, donor_weights,
         donor_receiver, target_stream, target_span):
    _, X, Z, Y = perturbation.shape
    donors = donor_stream.shape[1]
    cap = donors // 4
    slots = spans * cap
    assert Y == 128 and 2 * cap == 128 and rows > 2 and X % 4 == 0
    dma = pltpu.SemaphoreType.DMA
    finished = pl.pallas_call(
        functools.partial(kernel, rows, spans, X, Z, donors, cap),
        out_shape=jax.ShapeDtypeStruct(perturbation.shape, F32),
        in_specs=[pl.BlockSpec(memory_space=pl.ANY), pl.BlockSpec(memory_space=pl.ANY),
                  *[pl.BlockSpec(memory_space=pltpu.VMEM)] * 6],
        out_specs=pl.BlockSpec(memory_space=pl.ANY),
        scratch_shapes=[
            pltpu.VMEM((3, 5, X + 4, Z + 16, Y), F32),
            pltpu.VMEM((4, X, Z, Y), F32),
            pltpu.VMEM((5, spans, cap, Y), F32),
            pltpu.VMEM((3, 5, spans, cap, Y), F32),
            pltpu.VMEM((2, 5 * X * 2, Y), F32),
            pltpu.VMEM((3, 2, 5 * X * 2, Y), F32),
            pltpu.VMEM((spans, 8, 128), F32),
            pltpu.VMEM((spans, 8, 128), F32),
            pltpu.VMEM((2 * slots, X * Z), BF16),
            pltpu.VMEM((slots, Y), F32),
            pltpu.VMEM(((X - 8) * Z, slots), BF16),
            pltpu.VMEM((X, Z, Y), F32),
            pltpu.VMEM((8, slots), F32),
            pltpu.VMEM((X * Z, 2 * Y), BF16),
            pltpu.VMEM((2 * Y, 2 * Y), BF16),
            pltpu.VMEM((4, 5, Z, 2 * Y), F32),
            dma((6,)), dma((5,)), dma((5, spans)), dma((3, 5, spans)),
            dma((2,)), dma((3, 2)), dma((2,)), dma((3, 2)), dma((spans,)), dma((spans,)),
        ],
        compiler_params=pltpu.CompilerParams(
            collective_id=0, has_side_effects=True, vmem_limit_bytes=63 * 2**20),
    )(perturbation, base_flow, donor_stream, donor_span, donor_weights, donor_receiver,
      target_stream, target_span)
    return pl.pallas_call(
        deliver,
        out_shape=jax.ShapeDtypeStruct(perturbation.shape, F32),
        in_specs=[pl.BlockSpec(memory_space=pl.ANY)],
        out_specs=pl.BlockSpec(memory_space=pl.ANY),
        scratch_shapes=[pltpu.VMEM(perturbation.shape, F32), dma((10,)), dma((10,))],
        compiler_params=pltpu.CompilerParams(vmem_limit_bytes=63 * 2**20),
    )(finished)


def solution(mesh):
    in_specs = (
        P(None, "stream", "span", None),
        P(None, "stream", "span", None),
        P("stream", "span"),
        P("stream", "span"),
        P(None, "stream", "span"),
        P("stream", "span"),
        P("stream", "span"),
        P("stream", "span"),
    )
    out_specs = P(None, "stream", "span", None)
    part = functools.partial(body, mesh.shape["stream"], mesh.shape["span"])
    return jax.shard_map(part, mesh=mesh, in_specs=in_specs, out_specs=out_specs, check_vma=False)
```
